256 devices in a mesh: seq: 64 (over y, z, core), dp: 4 (over x).
Axes of the slice: x: 4, y: 4, z: 8, core: 2. Of those that a mesh axis runs over, the one named last changes fastest.
Arguments:
- features: bfloat16 [4, 131072, 192], P('dp', 'seq'), may hold values from -6 to 6
- grad_out: bfloat16 [4, 131072, 192], P('dp', 'seq'), may hold values from -6 to 6
- norm_gain: float32 [192], replicated, may hold values from 0.5 to 4
- w_qkv: bfloat16 [192, 576], replicated, may hold values from -0.4375 to 0.4375
- w_proj: bfloat16 [192, 192], replicated, may hold values from -0.4375 to 0.4375
- to_hilbert: int32 [4, 131072], P('dp', 'seq'), may hold values from 0 to 131071, as said below
- to_zorder: int32 [4, 131072], P('dp', 'seq'), may hold values from 0 to 131071, as said below
- counts: int32 [4, 128], P('dp', 'seq'), may hold values from 256 to 1024
Outputs:
- block_out: bfloat16 [4, 131072, 192], P('dp', 'seq')
- grad_features: bfloat16 [4, 131072, 192], P('dp', 'seq')
- grad_qkv: float32 [192, 576], replicated
- grad_proj: float32 [192, 192], replicated
- grad_gain: float32 [192], replicated
The draws below stay inside these ranges and needn't reach their ends.
Inputs may be any that keep to these rules, and one draw needn't show every extreme that they name: to_hilbert[s] is a permutation; each point's Hilbert position lies on the same index of seq as its Z position or on an adjacent one; at most 1024 points go from one index to an adjacent one, and in every slab exactly 1024 go from index 0 to index 1 and 1024 from index 1 to index 0. to_zorder[s] is the inverse permutation of to_hilbert[s].
All inputs are finite; a program needn't handle non-finite values.
Results may differ from the reference program's by a relative error of at most 0.006.
The reference program's roundings to bfloat16 on the way count: a program that leaves them out, or rounds other values in their place, can miss the bound.
Values may be sent and summed in bfloat16 or wider, within the bound.
A program may use at most 128 MiB of HBM per device.

```python
import jax
import jax.numpy as jnp
from jax import lax

C = 192
HEADS = 3
PATCH = 1024
P_DEV = 2048
SLABS = 4
NPTS = 131072
N_PATCH = 128


def draw_norm_gain(key, part):
    return jax.random.uniform(key, (C,), jnp.float32, 0.5, 1.5)


def permutation_pair(key):
    base_key = jax.random.fold_in(key, 11)
    devices = NPTS // P_DEV
    spill = P_DEV // 2

    def local_perm(one_key):
        return jax.random.permutation(one_key, P_DEV).astype(jnp.int32)

    def one_slab(slab_key):
        first_key, second_key, third_key = jax.random.split(slab_key, 3)
        crossing = jax.random.randint(third_key, (devices - 1,), 1, spill + 1, dtype=jnp.int32)
        crossing = crossing.at[0].set(spill)
        zero_one = jnp.zeros((1,), jnp.int32)
        left_cnt = jnp.concatenate([zero_one, crossing])[:, None]
        right_cnt = jnp.concatenate([crossing, zero_one])[:, None]
        order_in = jax.vmap(local_perm)(jax.random.split(first_key, devices))
        slots_out = jax.vmap(local_perm)(jax.random.split(second_key, devices))
        step_idx = jnp.arange(P_DEV, dtype=jnp.int32)[None, :]
        dev_idx = jnp.arange(devices, dtype=jnp.int32)[:, None]
        goes_left = step_idx < left_cnt
        goes_right = jnp.logical_and(step_idx >= left_cnt, step_idx < left_cnt + right_cnt)
        target = jnp.where(goes_left, dev_idx - 1, jnp.where(goes_right, dev_idx + 1, dev_idx))
        rank = jnp.where(goes_left, P_DEV - left_cnt + step_idx, jnp.where(goes_right, step_idx - left_cnt, step_idx - right_cnt))
        hilbert_pos = target * P_DEV + slots_out[target, rank]
        zorder_pos = dev_idx * P_DEV + order_in
        to_h = jnp.zeros((NPTS,), jnp.int32).at[zorder_pos.reshape(-1)].set(hilbert_pos.reshape(-1).astype(jnp.int32))
        to_z = jnp.zeros((NPTS,), jnp.int32).at[hilbert_pos.reshape(-1)].set(zorder_pos.reshape(-1).astype(jnp.int32))
        return (to_h, to_z)
    return jax.vmap(one_slab)(jax.random.split(base_key, SLABS))


def draw_to_hilbert(key, part):
    return permutation_pair(key)[0]


def draw_to_zorder(key, part):
    return permutation_pair(key)[1]


def draw_counts(key, part):
    drawn = jax.random.randint(key, (SLABS, N_PATCH), PATCH // 4, PATCH + 1, dtype=jnp.int32)
    drawn = drawn.at[:, 0].set(PATCH)
    return drawn.at[:, 1].set(PATCH // 4)


def shard_levels(rng, dims, cuts, low, high):
    gain = 1.0
    for axis_at, shards_of in cuts:
        heights = jax.random.uniform(jax.random.fold_in(jax.random.fold_in(rng, 6), axis_at), (shards_of,), jnp.float32, low / len(cuts), high / len(cuts))
        gain = gain * jnp.repeat(jnp.exp(heights), dims[axis_at] // shards_of).reshape((-1,) + (1,) * (len(dims) - 1 - axis_at))
    return gain


def bell_draw(key, extent, width, reach, pieces=(), held_as=jnp.bfloat16):
    gain = shard_levels(key, extent, pieces, -0.22, 0.18) if pieces else 1.0
    array = jax.random.normal(key, extent, jnp.float32) * width * gain
    return jnp.minimum(jnp.maximum(array, -reach), reach).astype(held_as)


def setup_inputs(seed: int = 0) -> dict:
    key_list = jax.random.split(jax.random.key(seed), 9)
    features = bell_draw(key_list[0], (SLABS, NPTS, C), 1.0, 6.0, ((0, 4), (1, 64)))
    grad_out = bell_draw(key_list[1], (SLABS, NPTS, C), 1.0, 6.0, ((0, 4), (1, 64)))
    norm_gain = draw_norm_gain(jax.random.fold_in(key_list[8], 71), 0)
    w_qkv = bell_draw(key_list[3], (C, 3 * C), C ** -0.5, 0.4375)
    w_proj = bell_draw(key_list[4], (C, C), C ** -0.5, 0.4375)
    to_hilbert = draw_to_hilbert(jax.random.fold_in(key_list[8], 71), 0)
    to_zorder = draw_to_zorder(jax.random.fold_in(key_list[8], 71), 0)
    counts = draw_counts(jax.random.fold_in(key_list[8], 71), 0)
    return dict(features=features, grad_out=grad_out, norm_gain=norm_gain, w_qkv=w_qkv, w_proj=w_proj, to_hilbert=to_hilbert, to_zorder=to_zorder, counts=counts)


EPS = 1e-05
NEG = -1e+30

def normalize(row_block, gain_vec):
    as_float = row_block.astype(jnp.float32)
    center = as_float - lax.optimization_barrier(jnp.mean(as_float, axis=-1, keepdims=True))
    inv_std = lax.rsqrt(lax.optimization_barrier(jnp.mean(center * center, axis=-1, keepdims=True)) + EPS)
    unit_rows = center * inv_std
    return (unit_rows, inv_std, (unit_rows * gain_vec).astype(jnp.bfloat16))

def patch_pass(x_patch, g_patch, unit_patch, inv_patch, normed_patch, live_count, gain_vec, w_qkv, w_proj):
    head_size = C // HEADS
    score_scale = head_size ** (-0.5)
    qkv_rows = jnp.dot(normed_patch, w_qkv, preferred_element_type=jnp.float32).astype(jnp.bfloat16)
    queries = qkv_rows[:, :C].reshape(PATCH, HEADS, head_size).astype(jnp.float32)
    keys_h = qkv_rows[:, C:2 * C].reshape(PATCH, HEADS, head_size).astype(jnp.float32)
    values_h = qkv_rows[:, 2 * C:].reshape(PATCH, HEADS, head_size).astype(jnp.float32)
    live_flag = jnp.arange(PATCH) < live_count
    scores = jnp.einsum('qhd,khd->hqk', queries, keys_h) * score_scale
    scores = jnp.where(live_flag[None, None, :], scores, NEG)
    highest = lax.optimization_barrier(jnp.max(scores, axis=-1, keepdims=True))
    weights = jnp.exp(scores - highest)
    attn_probs = weights / lax.optimization_barrier(jnp.sum(weights, axis=-1, keepdims=True))
    probs_bf16 = attn_probs.astype(jnp.bfloat16).astype(jnp.float32)
    attended = jnp.einsum('hqk,khd->qhd', probs_bf16, values_h).reshape(PATCH, C).astype(jnp.bfloat16)
    branch = jnp.dot(attended, w_proj, preferred_element_type=jnp.float32)
    live_mask = live_flag.astype(jnp.float32)[:, None]
    block_rows = (x_patch.astype(jnp.float32) + live_mask * branch).astype(jnp.bfloat16)
    g_masked = (g_patch.astype(jnp.float32) * live_mask).astype(jnp.bfloat16)
    grad_proj = jnp.dot(attended.T, g_masked, preferred_element_type=jnp.float32)
    d_attn = jnp.dot(g_masked, w_proj.T, preferred_element_type=jnp.float32).astype(jnp.bfloat16)
    d_attn = d_attn.reshape(PATCH, HEADS, head_size).astype(jnp.float32)
    d_probs = jnp.einsum('qhd,khd->hqk', d_attn, values_h)
    d_values = jnp.einsum('hqk,qhd->khd', probs_bf16, d_attn)
    row_delta = lax.optimization_barrier(jnp.sum(attn_probs * d_probs, axis=-1, keepdims=True))
    d_scores = (attn_probs * (d_probs - row_delta) * score_scale).astype(jnp.bfloat16).astype(jnp.float32)
    d_queries = jnp.einsum('hqk,khd->qhd', d_scores, keys_h)
    d_keys = jnp.einsum('hqk,qhd->khd', d_scores, queries)
    d_qkv = jnp.concatenate([d_queries.reshape(PATCH, C), d_keys.reshape(PATCH, C), d_values.reshape(PATCH, C)], axis=1).astype(jnp.bfloat16)
    grad_qkv = jnp.dot(normed_patch.T, d_qkv, preferred_element_type=jnp.float32)
    d_normed = jnp.dot(d_qkv, w_qkv.T, preferred_element_type=jnp.float32)
    grad_gain = lax.optimization_barrier(jnp.sum(unit_patch * d_normed, axis=0))
    d_unit = d_normed * gain_vec
    d_rows = inv_patch * (d_unit - lax.optimization_barrier(jnp.mean(d_unit, axis=-1, keepdims=True)) - unit_patch * lax.optimization_barrier(jnp.mean(d_unit * unit_patch, axis=-1, keepdims=True)))
    grad_rows = (g_patch.astype(jnp.float32) + d_rows).astype(jnp.bfloat16)
    return (block_rows, grad_rows, grad_qkv, grad_proj, grad_gain)

def reference(features, grad_out, norm_gain, w_qkv, w_proj, to_hilbert, to_zorder, counts):
    totals = (jnp.zeros((C, 3 * C), jnp.float32), jnp.zeros((C, C), jnp.float32), jnp.zeros((C,), jnp.float32))
    outputs_list = []
    grads_list = []
    for slab_idx in range(SLABS):
        x_hil = features[slab_idx][to_zorder[slab_idx]]
        g_hil = grad_out[slab_idx][to_zorder[slab_idx]]
        unit_rows, inv_std, normed = normalize(x_hil, norm_gain)

        def one_patch(running, patch_items):
            x_patch, g_patch, unit_patch, inv_patch, normed_patch, live_count = patch_items
            block_rows, grad_rows, grad_qkv, grad_proj, grad_gain = patch_pass(x_patch, g_patch, unit_patch, inv_patch, normed_patch, live_count, norm_gain, w_qkv, w_proj)
            return ((running[0] + grad_qkv, running[1] + grad_proj, running[2] + grad_gain), (block_rows, grad_rows))

        def by_patch(array_in):
            return array_in.reshape((-1, PATCH) + array_in.shape[1:])
        totals, (y_hil, dx_hil) = lax.scan(one_patch, totals, (by_patch(x_hil), by_patch(g_hil), by_patch(unit_rows), by_patch(inv_std), by_patch(normed), counts[slab_idx]))
        y_hil = y_hil.reshape(-1, C)
        dx_hil = dx_hil.reshape(-1, C)
        outputs_list.append(y_hil[to_hilbert[slab_idx]])
        grads_list.append(dx_hil[to_hilbert[slab_idx]])
    return (jnp.stack(outputs_list), jnp.stack(grads_list), totals[0], totals[1], totals[2])
```

```python
import functools

import jax
import jax.numpy as jnp
from jax import lax
from jax.experimental import pallas as pl
from jax.experimental.pallas import tpu as pltpu
from jax.sharding import PartitionSpec as P

HEADS = 3
PATCH = 1024
C = 192
D = 64
HP = 128
N = 2048
EPS = 1e-5
LOG2E = 1.4426950408889634
BF = jnp.bfloat16
F32 = jnp.float32
MESH = pl.DeviceIdType.MESH
VMEM_LIMIT = 60 * 2**20
GROUP = 16
TILES = 10


def dot(a, b):
    return jnp.dot(a, b, preferred_element_type=F32)


def dot_nt(a, b):
    return lax.dot_general(a, b, (((1,), (1,)), ((), ())), preferred_element_type=F32)


def dot_tn(a, b):
    return lax.dot_general(a, b, (((0,), (0,)), ((), ())), preferred_element_type=F32)


def gather_kernel(idx_ref, *refs):
    ins, outs, (src, dst) = refs[:6], refs[6:8], refs[8:]
    for i in range(3):
        for a in range(2):
            ref = ins[3 * a + i]

            def fill(t, c, ref=ref, i=i, a=a):
                rows = ref[pl.ds(t * 256, 256), :].astype(F32)
                at = i * 4 * N + t * 1024 + 2 * a
                src[pl.ds(at, 256, stride=4), :] = rows[:, :HP]
                tail = jnp.concatenate([rows[:, HP:], jnp.zeros((256, D), F32)], axis=1)
                src[pl.ds(at + 1, 256, stride=4), :] = tail
                return c

            lax.fori_loop(0, N // 256, fill, 0)

    def body(t, c):
        for u in range(16):
            j = t * 16 + u
            dst[pl.ds(pl.multiple_of(4 * j, 4), 4), :] = src[
                pl.ds(pl.multiple_of(idx_ref[j], 4), 4), :
            ]
        return c

    lax.fori_loop(0, N // 16, body, 0)

    for a in range(2):

        def out(t, c, a=a):
            at = t * 1024 + 2 * a
            head = dst[pl.ds(at, 256, stride=4), :]
            tail = dst[pl.ds(at + 1, 256, stride=4), :]
            outs[a][pl.ds(t * 256, 256), :] = jnp.concatenate([head, tail[:, :D]], axis=1).astype(BF)
            return c

        lax.fori_loop(0, N // 256, out, 0)


def gather(idx4, first, second):
    row = jax.ShapeDtypeStruct((N, C), BF)
    return pl.pallas_call(
        gather_kernel,
        out_shape=(row, row),
        in_specs=[pl.BlockSpec(memory_space=pltpu.SMEM)]
        + [pl.BlockSpec(memory_space=pltpu.VMEM)] * 6,
        scratch_shapes=[pltpu.VMEM((12 * N, HP), F32), pltpu.VMEM((4 * N, HP), F32)],
        compiler_params=pltpu.CompilerParams(vmem_limit_bytes=VMEM_LIMIT),
        name="rows",
    )(idx4, *first, *second)


def attn_kernel(
    QB,
    cnt_ref, x_ref, g_ref, gain_ref, wqkv_ref, wqkvT_ref, wproj_ref, wprojT_ref,
    y_ref, dx_ref, tot_ref,
    normed, qkv, dattn, attn, dqkv, dkacc, dvacc, gqkv, gproj, ggain,
):
    p = pl.program_id(0)
    live_n = cnt_ref[p]
    gain = gain_ref[...]
    x = x_ref[...].astype(F32)
    center = x - jnp.mean(x, axis=-1, keepdims=True)
    inv = lax.rsqrt(jnp.mean(center * center, axis=-1, keepdims=True) + EPS)
    unit = center * inv
    normed[...] = (unit * gain).astype(BF)
    row = lax.broadcasted_iota(jnp.int32, (PATCH, HP), 0)
    lane = lax.broadcasted_iota(jnp.int32, (PATCH, HP), 1)
    live = row[:, :1] < live_n
    livef = live.astype(F32)
    gl = jnp.where(live, g_ref[...].astype(F32), 0.0).astype(BF)
    nm = normed[...]
    bias = jnp.where(row < live_n, 0.0, -1e30)
    for h in range(HEADS):
        q = dot(nm, wqkv_ref[:, h * HP : (h + 1) * HP])
        q = q.astype(BF).astype(F32) * 0.125
        qkv[:, h * HP : (h + 1) * HP] = jnp.where(lane == D, 1.0, q).astype(BF)
        k = dot(nm, wqkv_ref[:, (3 + h) * HP : (4 + h) * HP])
        qkv[:, (3 + h) * HP : (4 + h) * HP] = jnp.where(lane == D, bias, k).astype(BF)
        v = dot(nm, wqkv_ref[:, (6 + h) * HP : (7 + h) * HP])
        qkv[:, (6 + h) * HP : (7 + h) * HP] = v.astype(BF)
        dattn[:, h * HP : (h + 1) * HP] = dot(gl, wprojT_ref[:, h * HP : (h + 1) * HP]).astype(BF)
    for h in range(HEADS):
        qq = slice(h * HP, (h + 1) * HP)
        kk = slice((3 + h) * HP, (4 + h) * HP)
        vv = slice((6 + h) * HP, (7 + h) * HP)
        k = qkv[:, kk]
        v = qkv[:, vv]
        for b in range(PATCH // QB):
            rs = slice(b * QB, (b + 1) * QB)
            qb = qkv[rs, qq]
            dob = dattn[rs, qq]
            s = dot_nt(qb, k)
            m = jnp.max(s, axis=-1, keepdims=True)
            e = jnp.exp2((s - m) * LOG2E)
            l = jnp.sum(e, axis=-1, keepdims=True)
            pn = e * (1.0 / l)
            pb = pn.astype(BF)
            o = dot(pb, v)
            attn[rs, qq] = o.astype(BF)
            dp = dot_nt(dob, v)
            delta = jnp.sum(o * dob.astype(F32), axis=-1, keepdims=True)
            ds = (pn * (dp - delta)).astype(BF)
            dqkv[rs, qq] = (dot(ds, k) * 0.125).astype(BF)
            dk = dot_tn(qb, ds)
            dv = dot_tn(dob, pb)
            if b == 0:
                dkacc[...] = dk
                dvacc[...] = dv
            else:
                dkacc[...] += dk
                dvacc[...] += dv
        dqkv[:, kk] = dkacc[...].T.astype(BF)
        dqkv[:, vv] = dvacc[...].T.astype(BF)
    at = attn[...]
    branch = dot(at, wproj_ref[...])
    y_ref[...] = (x + livef * branch).astype(BF)
    gp = dot_tn(at, gl)
    dq = dqkv[...]
    gq = dot_tn(nm, dq)
    dn = dot(dq, wqkvT_ref[...])
    gg = jnp.sum(unit * dn, axis=0, keepdims=True)
    du = dn * gain
    dr = inv * (
        du
        - jnp.mean(du, axis=-1, keepdims=True)
        - unit * jnp.mean(du * unit, axis=-1, keepdims=True)
    )
    dx_ref[...] = (g_ref[...].astype(F32) + dr).astype(BF)

    @pl.when(p == 0)
    def _():
        gqkv[...] = gq
        gproj[...] = gp
        ggain[...] = gg

    @pl.when(p != 0)
    def _():
        def half(i):
            return (gqkv[:, i * HP : i * HP + D] + gq[:, i * HP : i * HP + D]) if i < 9 else (
                jnp.concatenate(
                    [
                        gproj[h * HP : h * HP + D, (i - 9) * D : (i - 8) * D]
                        + gp[h * HP : h * HP + D, (i - 9) * D : (i - 8) * D]
                        for h in range(HEADS)
                    ],
                    axis=0,
                )
            )

        for ct in range(6):
            cols = jnp.concatenate([half(2 * ct), half(2 * ct + 1)], axis=1)
            for rt in range(24):
                t = rt * 6 + ct
                tot_ref[t // 9, t % 9, :, :] = cols[rt * 8 : (rt + 1) * 8, :]
        tot_ref[:, 9, :, :] = jnp.zeros((GROUP, 8, HP), F32)
        whole = ggain[...] + gg
        tot_ref[0, 9, 0:1, :] = whole[:, :HP]
        tot_ref[0, 9, 1:2, :D] = whole[:, HP:]


def pad_heads(w, n, axis):
    w = jnp.moveaxis(w, axis, -1)
    s = w.shape
    w = w.reshape(s[:-1] + (n, D))
    w = jnp.pad(w, [(0, 0)] * len(s[:-1]) + [(0, 0), (0, HP - D)])
    return jnp.moveaxis(w.reshape(s[:-1] + (n * HP,)), -1, axis)


def attn_call(cnt, x, g, gain, wqkv, wproj, QB=512):
    wq = pad_heads(wqkv, 9, 1)
    wp = pad_heads(wproj, 3, 0)

    def full(shape):
        return pl.BlockSpec(shape, lambda p: (0,) * len(shape))

    rows = pl.BlockSpec((PATCH, C), lambda p: (p, 0))
    return pl.pallas_call(
        functools.partial(attn_kernel, QB),
        grid=(2,),
        out_shape=(
            jax.ShapeDtypeStruct((N, C), BF),
            jax.ShapeDtypeStruct((N, C), BF),
            jax.ShapeDtypeStruct((GROUP, TILES, 8, HP), F32),
        ),
        in_specs=[
            pl.BlockSpec(memory_space=pltpu.SMEM),
            rows, rows,
            full((1, C)), full((C, 9 * HP)), full((9 * HP, C)), full((3 * HP, C)), full((C, 3 * HP)),
        ],
        out_specs=(rows, rows, full((GROUP, TILES, 8, HP))),
        scratch_shapes=[
            pltpu.VMEM((PATCH, C), BF), pltpu.VMEM((PATCH, 9 * HP), BF), pltpu.VMEM((PATCH, 3 * HP), BF),
            pltpu.VMEM((PATCH, 3 * HP), BF), pltpu.VMEM((PATCH, 9 * HP), BF),
            pltpu.VMEM((HP, PATCH), F32), pltpu.VMEM((HP, PATCH), F32),
            pltpu.VMEM((C, 9 * HP), F32), pltpu.VMEM((3 * HP, C), F32), pltpu.VMEM((1, C), F32),
        ],
        compiler_params=pltpu.CompilerParams(vmem_limit_bytes=VMEM_LIMIT),
        name="attention",
    )(cnt, x, g, gain.reshape(1, C), wq, wq.T, wp, wp.T)


def reduce_kernel(
    tot_ref, gqkv_ref, gproj_ref, ggain_ref,
    recv_a, sum_a, recv_b, fin, out_b, out_a,
    sa, ra, sb, rb, sc, rc, sd, rd,
):
    seq = lax.axis_index("seq")
    x = lax.axis_index("dp")
    y = seq // GROUP
    b = seq % GROUP
    a = y * 4 + x

    def dev_a(i):
        o = (a + i) % GROUP
        return o, {"dp": o % 4, "seq": (o // 4) * GROUP + b}

    def dev_b(i):
        o = (b + i) % GROUP
        return o, {"dp": x, "seq": y * GROUP + o}

    barrier = pltpu.get_barrier_semaphore()

    def greet(i, c):
        pl.semaphore_signal(barrier, inc=1, device_id=dev_a(i)[1], device_id_type=MESH)
        pl.semaphore_signal(barrier, inc=1, device_id=dev_b(i)[1], device_id_type=MESH)
        return c

    lax.fori_loop(1, GROUP, greet, 0)
    pl.semaphore_wait(barrier, 2 * (GROUP - 1))

    def loop(f, lo=1, hi=GROUP):
        def body(i, c):
            f(i)
            return c

        lax.fori_loop(lo, hi, body, 0)

    def copy_a(i):
        o, dev = dev_a(i)
        return pltpu.make_async_remote_copy(
            tot_ref.at[o], recv_a.at[a], sa.at[o], ra.at[a], device_id=dev, device_id_type=MESH
        )

    def into_a(o):
        return pltpu.make_async_remote_copy(
            tot_ref.at[o], recv_a.at[o], sa.at[o], ra.at[o],
            device_id=dev_a(1)[1], device_id_type=MESH,
        )

    recv_a[a] = tot_ref[a]
    loop(lambda i: copy_a(i).start())
    loop(lambda i: into_a((a + GROUP - i) % GROUP).wait_recv())
    acc = recv_a[0]
    for i in range(1, GROUP):
        acc = acc + recv_a[i]
    sum_a[...] = acc

    def copy_b(t):
        return pltpu.make_async_remote_copy(
            sum_a.at[t], recv_b.at[b], sb.at[t], rb.at[b],
            device_id={"dp": x, "seq": y * GROUP + t}, device_id_type=MESH,
        )

    def into_b(o):
        return pltpu.make_async_remote_copy(
            sum_a.at[0], recv_b.at[o], sb.at[0], rb.at[o],
            device_id=dev_b(1)[1], device_id_type=MESH,
        )

    def send_b(t):
        @pl.when(t != b)
        def _():
            copy_b(t).start()

    loop(send_b, 0, TILES)

    def copy_c(i):
        o, dev = dev_b(i)
        return pltpu.make_async_remote_copy(
            out_b.at[b], out_b.at[b], sc.at[o], rc.at[b], device_id=dev, device_id_type=MESH
        )

    def into_c(o):
        return pltpu.make_async_remote_copy(
            out_b.at[o], out_b.at[o], sc.at[o], rc.at[o],
            device_id=dev_b(1)[1], device_id_type=MESH,
        )

    @pl.when(b < TILES)
    def _():
        recv_b[b] = sum_a[b]
        loop(lambda i: into_b((b + GROUP - i) % GROUP).wait_recv())
        total = recv_b[0]
        for i in range(1, GROUP):
            total = total + recv_b[i]
        out_b[b] = total
        loop(lambda i: copy_c(i).start())

    def wait_c(t):
        @pl.when(t != b)
        def _():
            into_c(t).wait_recv()

    loop(wait_c, 0, TILES)

    def copy_d(i):
        o, dev = dev_a(i)
        return pltpu.make_async_remote_copy(
            out_b, out_a.at[a], sd.at[o], rd.at[a], device_id=dev, device_id_type=MESH
        )

    def into_d(o):
        return pltpu.make_async_remote_copy(
            out_b, out_a.at[o], sd.at[o], rd.at[o],
            device_id=dev_a(1)[1], device_id_type=MESH,
        )

    loop(lambda i: copy_d(i).start())
    out_a[a] = out_b[...]
    loop(lambda i: into_d((a + GROUP - i) % GROUP).wait_recv())

    def tile(rt, ct):
        t = rt * 6 + ct
        return out_a[t // 9, t % 9, :, :]

    for rt in range(24):
        rows = slice(rt * 8, (rt + 1) * 8)
        for ct in range(4):
            gqkv_ref[rows, ct * HP : (ct + 1) * HP] = tile(rt, ct)
        mid = tile(rt, 4)
        gqkv_ref[rows, 4 * HP :] = mid[:, :D]
        gproj_ref[rows, :] = jnp.concatenate([mid[:, D:], tile(rt, 5)], axis=1)
    ggain_ref[:, :HP] = out_a[0, 9, 0:1, :]
    ggain_ref[:, HP:] = out_a[0, 9, 1:2, :D]

    loop(lambda i: copy_a(i).wait_send())

    def sent_b(t):
        @pl.when(t != b)
        def _():
            copy_b(t).wait_send()

    loop(sent_b, 0, TILES)

    @pl.when(b < TILES)
    def _():
        loop(lambda i: copy_c(i).wait_send())

    loop(lambda i: copy_d(i).wait_send())


def reduce_all(tot):
    vmem = pl.BlockSpec(memory_space=pltpu.VMEM)
    return pl.pallas_call(
        reduce_kernel,
        out_shape=(
            jax.ShapeDtypeStruct((C, 3 * C), F32),
            jax.ShapeDtypeStruct((C, C), F32),
            jax.ShapeDtypeStruct((1, C), F32),
        ),
        in_specs=[vmem],
        out_specs=(vmem, vmem, vmem),
        scratch_shapes=[
            pltpu.VMEM((GROUP, TILES, 8, HP), F32),
            pltpu.VMEM((TILES, 8, HP), F32),
            pltpu.VMEM((GROUP, 8, HP), F32),
            pltpu.VMEM((8, HP), F32),
            pltpu.VMEM((TILES, 8, HP), F32),
            pltpu.VMEM((GROUP, TILES, 8, HP), F32),
        ]
        + [pltpu.SemaphoreType.DMA((GROUP,))] * 8,
        compiler_params=pltpu.CompilerParams(
            collective_id=0, has_side_effects=True, vmem_limit_bytes=VMEM_LIMIT
        ),
        name="reduce",
    )(tot)


def sides(v):
    peers = lax.axis_size("seq")
    up = [(i, i + 1) for i in range(peers - 1)]
    down = [(j, i) for i, j in up]
    return lax.ppermute(v, "seq", up), v, lax.ppermute(v, "seq", down)


def shards(features, grad_out, norm_gain, w_qkv, w_proj, to_hilbert, to_zorder, counts):
    base = (lax.axis_index("seq") - 1) * N
    x_hil, g_hil = gather((to_zorder[0] - base) * 4, sides(features[0]), sides(grad_out[0]))
    y_hil, dx_hil, tot = attn_call(counts[0], x_hil, g_hil, norm_gain, w_qkv, w_proj)
    grad_qkv, grad_proj, grad_gain = reduce_all(tot)
    y_zor, dx_zor = gather((to_hilbert[0] - base) * 4, sides(y_hil), sides(dx_hil))
    return (y_zor[None], dx_zor[None], grad_qkv, grad_proj, grad_gain[0])


def solution(mesh):
    rows = P("dp", "seq", None)
    in_specs = (rows, rows, P(), P(), P(), P("dp", "seq"), P("dp", "seq"), P("dp", "seq"))
    out_specs = (rows, rows, P(), P(), P())
    return jax.shard_map(shards, mesh=mesh, in_specs=in_specs, out_specs=out_specs, check_vma=False)
```

```python
import jax
import jax.numpy as jnp
from jax import lax
from jax.experimental import pallas as pl
from jax.experimental.pallas import tpu as pltpu
from jax.sharding import PartitionSpec as P

HEADS = 3
PATCH = 1024
PATCHES = 2
C = 192
D = 64
LANES = 128
N = 2048
QB = 256
EPS = 1e-5
LOG2E = 1.4426950408889634
BF = jnp.bfloat16
F32 = jnp.float32
MESH = pl.DeviceIdType.MESH
VMEM_LIMIT = 62 * 2**20
PLANE = 32
DEPTH = 8
TILES = 5
UNROLL = 16


def dot(a, b):
    return jnp.dot(a, b, preferred_element_type=F32)


def dot_nt(a, b):
    return lax.dot_general(a, b, (((1,), (1,)), ((), ())), preferred_element_type=F32)


def turned(a):
    return a.astype(F32).T.astype(a.dtype)


SCRATCH = dict(
    x_in=((C, N), BF), g_in=((C, N), BF),
    x_ext=((2, C, N), BF), g_ext=((2, C, N), BF),
    y_ext=((2, PATCHES, C, PATCH), BF), dx_ext=((2, PATCHES, C, PATCH), BF),
    x_hil=((PATCHES, C, PATCH), BF), g_hil=((PATCHES, C, PATCH), BF),
    y_hil=((PATCHES, C, PATCH), BF), dx_hil=((PATCHES, C, PATCH), BF),
    src=((4 * N * 2, LANES), F32), dst=((N * 2, LANES), F32),
    gain=((C, LANES), F32), w_qkv_t=((3 * C, C), BF), w_proj_t=((C, C), BF),
    inv=((PATCHES, 1, PATCH), F32), unit=((PATCHES, C, PATCH), F32),
    normed=((PATCHES, C, PATCH), BF), g_live=((PATCHES, C, PATCH), BF),
    q_ext=((HEADS, 2 * D, PATCH), BF), q_row=((HEADS, PATCH, D), BF),
    k_t=((HEADS, D, PATCH), BF), k_ext=((HEADS, PATCH, 2 * D), BF),
    v_t=((HEADS, D, PATCH), BF), v_row=((HEADS, PATCH, D), BF),
    do_t=((HEADS, D, PATCH), BF), do_row=((HEADS, PATCH, D), BF),
    attn=((PATCHES, C, PATCH), BF), d_qkv=((PATCHES, 3 * C, PATCH), BF),
    dk=((HEADS, PATCH, D), F32), dv=((HEADS, PATCH, D), F32),
    gq=((C, 3 * C), F32), gp=((C, C), F32),
    tot=((PLANE, TILES, 8, LANES), F32), recv_a=((PLANE, TILES, 8, LANES), F32),
    recv_z=((DEPTH, TILES, 8, LANES), F32), all_a=((PLANE, TILES, 8, LANES), F32),
)
SEMS = dict(
    in_sem=(2,), x_s=(2,), x_r=(2,), g_s=(2,), g_r=(2,),
    y_s=(2, PATCHES), y_r=(2, PATCHES), dx_s=(2, PATCHES), dx_r=(2, PATCHES),
    a_s=(PLANE,), a_r=(PLANE,), z_s=(DEPTH,), z_r=(DEPTH,), c_s=(PLANE,), c_r=(PLANE,),
)


class Refs:
    pass


def loop(lo, hi, f):
    def body(i, c):
        f(i)
        return c

    lax.fori_loop(lo, hi, body, 0)


def fill(r, at, cols):
    n = cols.shape[1]
    at = pl.multiple_of(at, n)
    cols = cols.astype(F32)
    r.src[pl.ds(2 * at, n, stride=2), :] = cols[:LANES].T
    tail = jnp.concatenate([cols[LANES:], jnp.zeros((2 * LANES - C, n), F32)], axis=0)
    r.src[pl.ds(2 * at + 1, n, stride=2), :] = tail.T


def fill_all(r, at, ref):
    def piece(t):
        fill(r, at + t * 512, ref[:, pl.ds(pl.multiple_of(t * 512, 512), 512)])

    loop(0, ref.shape[1] // 512, piece)


def pick(r, idx_ref):
    def rows(t):
        for u in range(UNROLL):
            j = t * UNROLL + u
            r.dst[pl.ds(pl.multiple_of(2 * j, 2), 2), :] = r.src[pl.ds(idx_ref[j], 2), :]

    loop(0, N // UNROLL, rows)


def picked(r, at, n):
    head = r.dst[pl.ds(2 * at, n, stride=2), :].T
    tail = r.dst[pl.ds(2 * at + 1, n, stride=2), :].T
    return jnp.concatenate([head, tail[: C - LANES]], axis=0).astype(BF)


def live_lanes(live_n):
    return lax.broadcasted_iota(jnp.int32, (1, PATCH), 1) < live_n


def prep_x(r, p):
    x = r.x_hil[p].astype(F32)
    center = x - jnp.mean(x, axis=0, keepdims=True)
    inv = lax.rsqrt(jnp.mean(center * center, axis=0, keepdims=True) + EPS)
    unit = center * inv
    r.inv[p] = inv
    r.unit[p] = unit
    r.normed[p] = (unit * r.gain[:, :1]).astype(BF)


def prep_heads(r, p, live_n):
    nm = r.normed[p]
    live = live_lanes(live_n)
    gl = jnp.where(live, r.g_hil[p].astype(F32), 0.0).astype(BF)
    r.g_live[p] = gl
    first = lax.broadcasted_iota(jnp.int32, (D, PATCH), 0) == 0
    bias = jnp.where(first, jnp.where(live, 0.0, -1e30), 0.0)
    ones = jnp.where(first, 1.0, 0.0).astype(BF)
    q = dot(r.w_qkv_t[:C, :], nm).astype(BF).astype(F32) * 0.125
    k = dot(r.w_qkv_t[C : 2 * C, :], nm).astype(BF).astype(F32)
    v = dot(r.w_qkv_t[2 * C :, :], nm).astype(BF).astype(F32)
    do = dot(r.w_proj[...], gl).astype(BF).astype(F32)
    for h in range(HEADS):
        hs = slice(h * D, (h + 1) * D)
        r.q_ext[h, :D, :] = q[hs].astype(BF)
        r.q_ext[h, D:, :] = ones
        r.q_row[h] = q[hs].T.astype(BF)
        r.k_t[h] = k[hs].astype(BF)
        r.k_ext[h] = jnp.concatenate([k[hs], bias], axis=0).T.astype(BF)
        r.v_t[h] = v[hs].astype(BF)
        r.v_row[h] = v[hs].T.astype(BF)
        r.do_t[h] = do[hs].astype(BF)
        r.do_row[h] = do[hs].T.astype(BF)


def core(r, p):
    blocks = PATCH // QB
    steps = [(h, b) for h in range(HEADS) for b in range(blocks)]

    def scores(i):
        h, b = steps[i]
        cs = slice(b * QB, (b + 1) * QB)
        return dot(r.k_ext[h], r.q_ext[h, :, cs]), dot(r.v_row[h], r.do_t[h, :, cs])

    def softmax(i, pair):
        h, b = steps[i]
        cs = slice(b * QB, (b + 1) * QB)
        s, dp = pair
        m = jnp.max(s, axis=0, keepdims=True)
        e = jnp.exp2((s - m) * LOG2E)
        pn = e * (1.0 / jnp.sum(e, axis=0, keepdims=True))
        pb = pn.astype(BF)
        o = dot(r.v_t[h], pb)
        r.attn[p, h * D : (h + 1) * D, cs] = o.astype(BF)
        delta = jnp.sum(o * r.do_t[h, :, cs].astype(F32), axis=0, keepdims=True)
        return pb, (pn * (dp - delta)).astype(BF)

    def grads(i, pair):
        h, b = steps[i]
        cs = slice(b * QB, (b + 1) * QB)
        pb, ds = pair
        r.d_qkv[p, h * D : (h + 1) * D, cs] = (dot(r.k_t[h], ds) * 0.125).astype(BF)
        dk = dot(ds, r.q_row[h, cs, :])
        dv = dot(pb, r.do_row[h, cs, :])
        if b:
            dk = r.dk[h] + dk
            dv = r.dv[h] + dv
        if b < blocks - 1:
            r.dk[h] = dk
            r.dv[h] = dv
        else:
            r.d_qkv[p, C + h * D : C + (h + 1) * D, :] = dk.T.astype(BF)
            r.d_qkv[p, 2 * C + h * D : 2 * C + (h + 1) * D, :] = dv.T.astype(BF)

    ahead = scores(0)
    behind = None
    for i in range(len(steps)):
        now = ahead
        ahead = scores(i + 1) if i + 1 < len(steps) else None
        pair = softmax(i, now)
        if behind is not None:
            grads(i - 1, behind)
        behind = pair
    grads(len(steps) - 1, behind)


def weight_grads(r, p):
    return dot_nt(r.normed[p], r.d_qkv[p]), dot_nt(r.attn[p], r.g_live[p])


def block_rows(r, p, live_n):
    livef = jnp.where(live_lanes(live_n), 1.0, 0.0)
    branch = dot(r.w_proj_t[...], r.attn[p])
    r.y_hil[p] = (r.x_hil[p].astype(F32) + livef * branch).astype(BF)


def feature_grads(r, p):
    du = dot(r.w_qkv[...], r.d_qkv[p]) * r.gain[:, :1]
    unit = r.unit[p]
    dr = r.inv[p] * (
        du
        - jnp.mean(du, axis=0, keepdims=True)
        - unit * jnp.mean(du * unit, axis=0, keepdims=True)
    )
    r.dx_hil[p] = (r.g_hil[p].astype(F32) + dr).astype(BF)


def kernel(
    cnt_ref, zor_ref, hil_ref, x_hbm, g_hbm, gain_ref, wqkv_ref, wproj_ref,
    y_ref, dx_ref, gqkv_ref, gproj_ref, ggain_ref, *scratch,
):
    r = Refs()
    for name, ref in zip(list(SCRATCH) + list(SEMS), scratch):
        setattr(r, name, ref)
    r.w_qkv, r.w_proj = wqkv_ref, wproj_ref
    seq = lax.axis_index("seq")
    x_at = lax.axis_index("dp")
    last = lax.axis_size("seq") - 1
    y_at = seq // 16
    z_at = (seq // 2) % 8
    core_at = seq % 2
    a = (y_at * 4 + x_at) * 2 + core_at
    home = (seq % 4) * N
    sides = (((seq + 3) % 4) * N, ((seq + 1) % 4) * N)

    def plane(o):
        return {"dp": (o // 2) % 4, "seq": (o // 8) * 16 + z_at * 2 + o % 2}

    def depth(o):
        return {"dp": x_at, "seq": y_at * 16 + o * 2 + core_at}

    barrier = pltpu.get_barrier_semaphore()

    def greet(dev):
        pl.semaphore_signal(barrier, inc=1, device_id=dev, device_id_type=MESH)

    has_left = seq > 0
    has_right = seq < last

    @pl.when(has_left)
    def _():
        greet({"seq": seq - 1})

    @pl.when(has_right)
    def _():
        greet({"seq": seq + 1})

    loop(1, PLANE, lambda i: greet(plane((a + i) % PLANE)))
    loop(1, DEPTH, lambda i: greet(depth((z_at + i) % DEPTH)))

    x_copy = pltpu.make_async_copy(x_hbm, r.x_in, r.in_sem.at[0])
    g_copy = pltpu.make_async_copy(g_hbm, r.g_in, r.in_sem.at[1])
    x_copy.start()
    g_copy.start()
    peers = PLANE - 1 + DEPTH - 1
    inner = jnp.logical_and(has_left, has_right)

    @pl.when(inner)
    def _():
        pl.semaphore_wait(barrier, peers + 2)

    @pl.when(jnp.logical_not(inner))
    def _():
        pl.semaphore_wait(barrier, peers + 1)

    def to_left(ref, ext, ss, rs, *at):
        return pltpu.make_async_remote_copy(
            ref, ext.at[(1,) + at], ss.at[(1,) + at], rs.at[(1,) + at],
            device_id={"seq": seq - 1}, device_id_type=MESH,
        )

    def to_right(ref, ext, ss, rs, *at):
        return pltpu.make_async_remote_copy(
            ref, ext.at[(0,) + at], ss.at[(0,) + at], rs.at[(0,) + at],
            device_id={"seq": seq + 1}, device_id_type=MESH,
        )

    def send(*args):
        @pl.when(has_left)
        def _():
            to_left(*args).start()

        @pl.when(has_right)
        def _():
            to_right(*args).start()

    def received(ref, ext, ss, rs, *at):
        def arrival(slot, peer):
            return pltpu.make_async_remote_copy(
                ref, ext.at[(slot,) + at], ss.at[(slot,) + at], rs.at[(slot,) + at],
                device_id={"seq": peer}, device_id_type=MESH,
            )

        @pl.when(has_left)
        def _():
            arrival(0, seq - 1).wait_recv()

        @pl.when(has_right)
        def _():
            arrival(1, seq + 1).wait_recv()

    def sent(*args):
        @pl.when(has_left)
        def _():
            to_left(*args).wait_send()

        @pl.when(has_right)
        def _():
            to_right(*args).wait_send()

    x_args = (x_hbm, r.x_ext, r.x_s, r.x_r)
    g_args = (g_hbm, r.g_ext, r.g_s, r.g_r)

    def y_args(p):
        return (r.y_hil.at[p], r.y_ext, r.y_s, r.y_r, p)

    def dx_args(p):
        return (r.dx_hil.at[p], r.dx_ext, r.dx_s, r.dx_r, p)

    send(*x_args)
    r.w_qkv_t[...] = turned(wqkv_ref[...])
    r.w_proj_t[...] = turned(wproj_ref[...])
    r.gain[...] = jnp.broadcast_to(gain_ref[...], (LANES, C)).T
    x_copy.wait()
    g_copy.wait()
    fill_all(r, home, r.x_in)
    received(*x_args)
    send(*g_args)
    fill_all(r, sides[0], r.x_ext.at[0])
    fill_all(r, sides[1], r.x_ext.at[1])
    pick(r, zor_ref)

    def take_x(p):
        r.x_hil[p] = picked(r, p * PATCH, PATCH)
        prep_x(r, p)

    loop(0, PATCHES, take_x)
    fill_all(r, home, r.g_in)
    received(*g_args)
    fill_all(r, sides[0], r.g_ext.at[0])
    fill_all(r, sides[1], r.g_ext.at[1])
    pick(r, zor_ref)

    def take_g(p):
        r.g_hil[p] = picked(r, p * PATCH, PATCH)

    loop(0, PATCHES, take_g)

    prep_heads(r, 0, cnt_ref[0])
    core(r, 0)
    gq, gp = weight_grads(r, 0)
    r.gq[...] = gq
    r.gp[...] = gp
    block_rows(r, 0, cnt_ref[0])
    send(*y_args(0))
    feature_grads(r, 0)
    send(*dx_args(0))

    prep_heads(r, 1, cnt_ref[1])
    core(r, 1)
    gq, gp = weight_grads(r, 1)
    whole = jnp.concatenate([r.gq[...] + gq, r.gp[...] + gp], axis=1)
    for rt in range(C // 8):
        for ct in range(6):
            t = rt * 6 + ct
            r.tot[t // TILES, t % TILES, :, :] = whole[
                rt * 8 : (rt + 1) * 8, ct * LANES : (ct + 1) * LANES
            ]
    for t in range(144, PLANE * TILES):
        r.tot[t // TILES, t % TILES, :, :] = jnp.zeros((8, LANES), F32)

    def copy_a(o):
        return pltpu.make_async_remote_copy(
            r.tot.at[o], r.recv_a.at[a], r.a_s.at[o], r.a_r.at[a],
            device_id=plane(o), device_id_type=MESH,
        )

    def into_a(o):
        return pltpu.make_async_remote_copy(
            r.tot.at[o], r.recv_a.at[o], r.a_s.at[o], r.a_r.at[o],
            device_id=plane(o), device_id_type=MESH,
        )

    def copy_z(o):
        return pltpu.make_async_remote_copy(
            r.recv_z.at[z_at], r.recv_z.at[z_at], r.z_s.at[o], r.z_r.at[z_at],
            device_id=depth(o), device_id_type=MESH,
        )

    def into_z(o):
        return pltpu.make_async_remote_copy(
            r.recv_z.at[o], r.recv_z.at[o], r.z_s.at[o], r.z_r.at[o],
            device_id=depth(o), device_id_type=MESH,
        )

    def copy_c(o):
        return pltpu.make_async_remote_copy(
            r.all_a.at[a], r.all_a.at[a], r.c_s.at[o], r.c_r.at[a],
            device_id=plane(o), device_id_type=MESH,
        )

    def into_c(o):
        return pltpu.make_async_remote_copy(
            r.all_a.at[o], r.all_a.at[o], r.c_s.at[o], r.c_r.at[o],
            device_id=plane(o), device_id_type=MESH,
        )

    def in_plane(f):
        loop(1, PLANE, lambda i: f((a + i) % PLANE))

    def in_depth(f):
        loop(1, DEPTH, lambda i: f((z_at + i) % DEPTH))

    in_plane(lambda o: copy_a(o).start())
    r.recv_a[a] = r.tot[a]

    block_rows(r, 1, cnt_ref[1])
    send(*y_args(1))
    feature_grads(r, 1)
    send(*dx_args(1))

    def own(ref):
        fill(r, home, ref[0])
        fill(r, home + PATCH, ref[1])

    def side(slot, ext, p):
        fill(r, sides[slot] + p * PATCH, ext[slot, p])

    received(*y_args(0))
    own(r.y_hil)
    side(0, r.y_ext, 0)
    side(1, r.y_ext, 0)

    in_plane(lambda o: into_a(o).wait_recv())
    acc = r.recv_a[0]
    for i in range(1, PLANE):
        acc = acc + r.recv_a[i]
    r.recv_z[z_at] = acc
    in_depth(lambda o: copy_z(o).start())

    received(*y_args(1))
    side(0, r.y_ext, 1)
    side(1, r.y_ext, 1)
    pick(r, hil_ref)

    in_depth(lambda o: into_z(o).wait_recv())
    acc = r.recv_z[0]
    for i in range(1, DEPTH):
        acc = acc + r.recv_z[i]
    r.all_a[a] = acc
    in_plane(lambda o: copy_c(o).start())

    def put(ref):
        def piece(t):
            at = pl.multiple_of(t * 512, 512)
            ref[:, pl.ds(at, 512)] = picked(r, t * 512, 512)

        loop(0, N // 512, piece)

    put(y_ref)
    received(*dx_args(0))
    received(*dx_args(1))
    own(r.dx_hil)
    for p in range(PATCHES):
        side(0, r.dx_ext, p)
        side(1, r.dx_ext, p)
    pick(r, hil_ref)
    put(dx_ref)

    in_plane(lambda o: into_c(o).wait_recv())

    def tile(rt, ct):
        t = rt * 6 + ct
        return r.all_a[t // TILES, t % TILES, :, :]

    for rt in range(C // 8):
        rows = slice(rt * 8, (rt + 1) * 8)
        for ct in range(4):
            gqkv_ref[rows, ct * LANES : (ct + 1) * LANES] = tile(rt, ct)
        mid = tile(rt, 4)
        gqkv_ref[rows, 4 * LANES :] = mid[:, :D]
        gproj_ref[rows, :] = jnp.concatenate([mid[:, D:], tile(rt, 5)], axis=1)
    gg = jnp.sum(gqkv_ref[...] * wqkv_ref[...].astype(F32), axis=1, keepdims=True)
    gg = jnp.broadcast_to(gg, (C, LANES)) / r.gain[...]
    ggain_ref[...] = gg.T[:1, :]

    sent(*x_args)
    sent(*g_args)
    for p in range(PATCHES):
        sent(*y_args(p))
        sent(*dx_args(p))
    in_plane(lambda o: copy_a(o).wait_send())
    in_depth(lambda o: copy_z(o).wait_send())
    in_plane(lambda o: copy_c(o).wait_send())


def place(index):
    return (index[0] % (4 * N)) * 2


def hand_out(*refs):
    for i in range(5):
        refs[5 + i][...] = refs[i][...]


def shards(features, grad_out, norm_gain, w_qkv, w_proj, to_hilbert, to_zorder, counts):
    vmem = pl.BlockSpec(memory_space=pltpu.VMEM)
    smem = pl.BlockSpec(memory_space=pltpu.SMEM)
    hbm = pl.BlockSpec(memory_space=pl.ANY)
    made = pl.pallas_call(
        kernel,
        out_shape=(
            jax.ShapeDtypeStruct((C, N), BF),
            jax.ShapeDtypeStruct((C, N), BF),
            jax.ShapeDtypeStruct((C, 3 * C), F32),
            jax.ShapeDtypeStruct((C, C), F32),
            jax.ShapeDtypeStruct((1, C), F32),
        ),
        in_specs=[smem, smem, smem, hbm, hbm, vmem, vmem, vmem],
        out_specs=(vmem,) * 5,
        scratch_shapes=[pltpu.VMEM(s, d) for s, d in SCRATCH.values()]
        + [pltpu.SemaphoreType.DMA(s) for s in SEMS.values()],
        compiler_params=pltpu.CompilerParams(
            collective_id=0, has_side_effects=True, vmem_limit_bytes=VMEM_LIMIT
        ),
        name="block",
    )(
        counts[0], place(to_zorder), place(to_hilbert), features[0].T, grad_out[0].T,
        norm_gain.reshape(1, C), w_qkv, w_proj,
    )
    y, dx, gqkv, gproj, ggain = pl.pallas_call(
        hand_out,
        out_shape=[jax.ShapeDtypeStruct(m.shape, m.dtype) for m in made],
        in_specs=[vmem] * 5,
        out_specs=[vmem] * 5,
        name="hand_out",
    )(*made)
    return (y.T[None], dx.T[None], gqkv, gproj, ggain[0])


def solution(mesh):
    rows = P("dp", "seq", None)
    in_specs = (rows, rows, P(), P(), P(), P("dp", "seq"), P("dp", "seq"), P("dp", "seq"))
    out_specs = (rows, rows, P(), P(), P())
    return jax.shard_map(shards, mesh=mesh, in_specs=in_specs, out_specs=out_specs, check_vma=False)
```
